32 devices in a mesh: grp: 2 (over y), run: 4 (over x, core), chan: 4 (over z).
Axes of the slice: x: 2, y: 2, z: 4, core: 2. Of those that a mesh axis runs over, the one named last changes fastest.
Arguments:
- embed: bfloat16 [512, 8192], P('grp', 'chan'), parts along dimension 0, may hold values from -6 to 6
- noise: bfloat16 [16, 32, 8192], P(('grp', 'run'), None, 'chan'), parts along dimension 0, may hold values from -12 to 12
- positions: int32 [16, 32], P(('grp', 'run')), parts along dimension 0, may hold values from 0 to 255
- restore: int32 [16, 2], P(('grp', 'run')), parts along dimension 0, may hold values 0 or 1
- short_one: float32 [7, 8192], P(None, 'chan'), may hold values from -2 to 2
- long_one: float32 [128, 8192], P(None, 'chan'), may hold values from -0.5 to 0.5
- out_weight: bfloat16 [8192, 8192], P(None, 'chan'), may hold values from -0.0625 to 0.0625
- short_two: float32 [7, 8192], P(None, 'chan'), may hold values from -2 to 2
- long_two: float32 [128, 8192], P(None, 'chan'), may hold values from -0.5 to 0.5
Outputs:
- traced: bfloat16 [16, 256, 8192], P(('grp', 'run'), None, 'chan'), parts along dimension 0
The draws below stay inside these ranges and needn't reach their ends.
There are 2 independent parts, one for each index of `grp`. The reference program is written for one: setup_inputs(seed, part) draws one part's arguments, and reference() takes and returns one part's arrays. A program takes and returns all parts, laid end to end along the dimension named above; an argument that names none is the same for every part. Nothing has to cross between parts.
All inputs are finite; a program needn't handle non-finite values. No bound on the sum of `restore` on one device may be relied on, other than what follows from the above.
Results may differ from the reference program's by a relative error of at most 0.007.
Values may be sent and summed in bfloat16 or wider, within the bound.
A program may use at most 128 MiB of HBM per device.

```python
import math
import jax
import jax.numpy as jnp
from jax import lax

D = 8192
SEQ = 256
TAPS = 128
SHORT = 7
RUNS = 8
NBLK = 2
NCOR = 32


def touch_ends(values, rng, smallest, high):
    spot = [jax.random.randint(jax.random.fold_in(rng, axis), (), 0, length) for axis, length in enumerate(values.shape)]
    longest = values.shape.index(max(values.shape))
    neighbour = spot[:longest] + [(spot[longest] + 1) % values.shape[longest]] + spot[longest + 1:]
    return values.at[tuple(spot)].set(smallest).at[tuple(neighbour)].set(high)


def block_scale(key, extent, shards, low, largest):
    gain, own = 1.0, jax.random.fold_in(key, 6)
    for dim, blocks in shards:
        steps = jnp.exp(jax.random.uniform(jax.random.fold_in(own, dim), (blocks,), jnp.float32, low / len(shards), largest / len(shards)))
        gain = gain * jnp.repeat(steps, extent[dim] // blocks).reshape([-1 if axis == dim else 1 for axis in range(len(extent))])
    return gain


def bell_draw(rng, shape, spread, bound, cuts=(), kind=jnp.bfloat16):
    values = jax.random.normal(rng, shape, jnp.float32) * spread
    if len(cuts) > 0:
        values = block_scale(rng, shape, cuts, -0.22, 0.18) * values
    return jnp.clip(values, min=-bound, max=bound).astype(kind)


def setup_inputs(seed: int = 0, part: int = 0) -> dict:
    streams_of = jax.random.split(jax.random.key(seed), 10)
    part_keys = jax.random.split(jax.random.fold_in(streams_of[9], part), 10)
    return {
        "embed": bell_draw(part_keys[0], (SEQ, D), 1.0, 6.0, ((1, 4),)),
        "noise": bell_draw(part_keys[1], (RUNS, NCOR, D), 3.0, 12.0, ((0, 4), (2, 4))),
        "positions": touch_ends(jax.random.randint(part_keys[2], (RUNS, NCOR), 0, SEQ), jax.random.fold_in(part_keys[2], 1), 0, SEQ - 1).astype(jnp.int32),
        "restore": touch_ends((jax.random.randint(part_keys[3], (RUNS, NBLK), 0, 2) < 1).astype(jnp.int32), jax.random.fold_in(part_keys[3], 1), 0, 1),
        "short_one": bell_draw(streams_of[4], (SHORT, D), SHORT ** -0.5, 2.0, ((1, 4),), jnp.float32),
        "long_one": bell_draw(streams_of[5], (TAPS, D), TAPS ** -0.5, 0.5, ((1, 4),), jnp.float32),
        "out_weight": bell_draw(streams_of[6], (D, D), D ** -0.5, 0.0625, ((1, 4),)),
        "short_two": bell_draw(streams_of[7], (SHORT, D), SHORT ** -0.5, 2.0, ((1, 4),), jnp.float32),
        "long_two": bell_draw(streams_of[8], (TAPS, D), TAPS ** -0.5, 0.5, ((1, 4),), jnp.float32),
    }


block_rows = 32


def short_filter(field, filter_taps):
    length = field.shape[1]
    running = jnp.zeros(field.shape, jnp.float32)
    for shift_count in range(filter_taps.shape[0]):
        shifted = jnp.pad(field, ((0, 0), (shift_count, 0), (0, 0)))[:, :length]
        running = running + filter_taps[shift_count][None, None, :] * shifted
    return running


def block_filter(field, filter_taps):
    runs_here, length, width = field.shape
    span = filter_taps.shape[0]
    rows = min(block_rows, length)
    blocks = length // rows
    reach = span // rows
    padded = jnp.pad(field, ((0, 0), (span, 0), (0, 0))).reshape(runs_here, blocks + reach, rows, width)
    windows = jnp.concatenate([padded[:, offset:offset + blocks] for offset in range(reach + 1)], axis=2)
    group = math.gcd(width, 128)
    groups = width // group
    windows = windows.reshape(runs_here, blocks, span + rows, groups, group).transpose(3, 0, 1, 2, 4)
    grouped_taps = filter_taps.reshape(span, groups, group).transpose(1, 0, 2)
    row_index = jnp.arange(rows, dtype=jnp.int32)[:, None]
    col_index = jnp.arange(span + rows, dtype=jnp.int32)[None, :]
    lag_index = row_index + span - col_index
    valid = (lag_index >= 0) & (lag_index < span)
    clipped = jnp.clip(lag_index, 0, span - 1)

    def one_group(operands):
        window_group, taps_group = operands
        table = jnp.where(valid[:, :, None], taps_group[clipped], jnp.float32(0.0))
        return jnp.einsum("ijc,rbjc->rbic", table, window_group, precision=lax.Precision.HIGHEST)

    result = lax.map(one_group, (windows, grouped_taps))
    return result.transpose(1, 2, 3, 0, 4).reshape(runs_here, length, width)


def reference(embed, noise, positions, restore, short_one, long_one, out_weight, short_two, long_two):
    runs_all = noise.shape[0]
    length, width = embed.shape
    onehot = (jnp.arange(length, dtype=jnp.int32)[None, :, None] == positions[:, None, :]).astype(jnp.float32)
    added = jnp.einsum("rlp,rpc->rlc", onehot, noise.astype(jnp.float32), precision=lax.Precision.HIGHEST)
    corrupt_flag = (jnp.arange(runs_all, dtype=jnp.int32) != 0).astype(jnp.float32)[:, None, None]
    inputs = (embed.astype(jnp.float32)[None] + corrupt_flag * added).astype(jnp.bfloat16)
    input_values = inputs.astype(jnp.float32)
    filtered = block_filter(short_filter(input_values, short_one), long_one)
    mixed = (filtered * jax.nn.silu(input_values)).astype(jnp.bfloat16)
    projected = jnp.dot(mixed.reshape(runs_all * length, width), out_weight, preferred_element_type=jnp.float32)
    hidden = (input_values + projected.reshape(runs_all, length, width)).astype(jnp.bfloat16)
    block_size = length // restore.shape[1]
    restored_rows = jnp.repeat(restore, block_size, axis=1)[:, :, None] == 1
    restored = jnp.where(restored_rows, hidden[0][None], hidden)
    restored_values = restored.astype(jnp.float32)
    second = block_filter(short_filter(restored_values, short_two), long_two)
    return (restored_values + second * jax.nn.silu(restored_values)).astype(jnp.bfloat16)
```

```python
import functools

import jax
import jax.numpy as jnp
import numpy as np
from jax import lax
from jax.experimental import pallas as pl
from jax.experimental.pallas import tpu as pltpu
from jax.sharding import PartitionSpec as P


def transform_tables(length, taps_rows, size):
    half = size // 2
    angle = 2.0 * np.pi * (np.arange(half)[:, None] + 0.5) / size
    field = angle * np.arange(length)[None, :]
    taps = angle * np.arange(taps_rows)[None, :]
    forward = np.concatenate([np.cos(field), -np.sin(field)], axis=0)
    taps_forward = np.concatenate([np.cos(taps), -np.sin(taps)], axis=0)
    inverse = np.concatenate([np.cos(field), -np.sin(field)], axis=0).T * (2.0 / size)
    kinds = [jnp.asarray(table, dtype=jnp.bfloat16) for table in (forward, taps_forward, inverse)]
    return kinds


def dot(left, right):
    return jnp.dot(left, right, preferred_element_type=jnp.float32)


def gate(values):
    return 0.5 * values * (1.0 + jnp.tanh(0.5 * values))


def spectral_filter(field, spectrum_re, spectrum_im, forward, inverse):
    half = spectrum_re.shape[0]
    field_spectrum = dot(forward, field)
    re, im = field_spectrum[:half], field_spectrum[half:]
    out_re = (re * spectrum_re - im * spectrum_im).astype(jnp.bfloat16)
    out_im = (re * spectrum_im + im * spectrum_re).astype(jnp.bfloat16)
    return dot(inverse[:, :half], out_re) + dot(inverse[:, half:], out_im)


def project_kernel(
    embed, noise, onehot, taps, weight, forward, taps_forward, inverse, out
):
    step = pl.program_id(0)
    runs = noise.shape[1]
    length = embed.shape[1]
    half = forward.shape[0] // 2
    spectrum = dot(taps_forward[...], taps[0])
    spectrum_re, spectrum_im = spectrum[:half], spectrum[half:]

    @pl.when(step == 0)
    def _():
        out[...] = jnp.zeros_like(out)

    base = embed[0]
    for r in range(runs + 1):
        if r < runs:
            added = dot(onehot[r], noise[0, r])
            field = (base.astype(jnp.float32) + added).astype(jnp.bfloat16)
        else:
            field = base
        filtered = spectral_filter(
            field, spectrum_re, spectrum_im, forward[...], inverse[...]
        )
        mixed = (filtered * gate(field.astype(jnp.float32))).astype(jnp.bfloat16)
        rows = pl.ds(r * length, length)
        out[rows] += dot(mixed, weight[...])


def second_kernel(
    embed, noise, onehot, restore, taps, projected, forward, taps_forward, inverse, out
):
    runs = noise.shape[0]
    length = embed.shape[0]
    half = forward.shape[0] // 2
    spectrum = dot(taps_forward[...], taps[...])
    spectrum_re, spectrum_im = spectrum[:half], spectrum[half:]
    base = embed[...].astype(jnp.float32)
    clean = (base + projected[pl.ds(runs * length, length)]).astype(jnp.bfloat16)
    for r in range(runs):
        added = dot(onehot[r], noise[r])
        field = (base + added).astype(jnp.bfloat16).astype(jnp.float32)
        hidden = (field + projected[pl.ds(r * length, length)]).astype(jnp.bfloat16)
        flags = restore[r]
        values = jnp.where(flags == 1, clean.astype(jnp.float32), hidden.astype(jnp.float32))
        second = spectral_filter(
            values.astype(jnp.bfloat16), spectrum_re, spectrum_im, forward[...], inverse[...]
        )
        out[r] = (values + second * gate(values)).astype(jnp.bfloat16)


def combined_taps(short_taps, long_taps, rows):
    total = jnp.zeros((rows, long_taps.shape[1]), jnp.float32)
    for k in range(short_taps.shape[0]):
        shifted = jnp.pad(long_taps, ((k, rows - k - long_taps.shape[0]), (0, 0)))
        total = total + short_taps[k][None, :] * shifted
    return total.astype(jnp.bfloat16)


def whole(shape):
    return pl.BlockSpec(shape, lambda *_: (0,) * len(shape))


def per_device(
    embed, noise, positions, restore, short_one, long_one, out_weight, short_two, long_two
):
    runs, corrupted, width = noise.shape
    length = embed.shape[0]
    chan_count = lax.axis_size("chan")
    run_devices = lax.axis_size("run")
    run_index = lax.axis_index("run")
    run_ids = run_index * runs + jnp.arange(runs, dtype=jnp.int32)
    span = short_one.shape[0] + long_one.shape[0] - 1
    unit = 8 * run_devices
    taps_rows = -(-span // unit) * unit
    size = 512
    assert length + span - 1 <= size
    forward, taps_forward, inverse = transform_tables(length, taps_rows, size)

    onehot = (
        (jnp.arange(length, dtype=jnp.int32)[None, :, None] == positions[:, None, :])
        & (run_ids != 0)[:, None, None]
    ).astype(jnp.bfloat16)
    block_size = length // restore.shape[1]
    flags = jnp.repeat(restore, block_size, axis=1)[:, :, None]

    taps_one = combined_taps(short_one, long_one, taps_rows)
    taps_two = combined_taps(short_two, long_two, taps_rows)

    piece = jnp.concatenate(
        [
            lax.dynamic_slice_in_dim(
                embed, run_index * (length // run_devices), length // run_devices, axis=0
            ),
            lax.dynamic_slice_in_dim(
                taps_one, run_index * (taps_rows // run_devices), taps_rows // run_devices, axis=0
            ),
        ],
        axis=0,
    )
    shared = lax.all_gather(piece, ("chan", "run"), axis=0)
    rows_here = length // run_devices
    all_embed = shared[:, :rows_here].reshape(chan_count, length, width)
    all_taps = shared[:, rows_here:].reshape(chan_count, taps_rows, width)
    all_noise = lax.all_gather(noise, "chan", axis=0)

    tile = min(512, width)
    per = width // tile
    tables = [forward, taps_forward, inverse]
    table_specs = [whole(table.shape) for table in tables]
    projected = pl.pallas_call(
        project_kernel,
        grid=(chan_count * per,),
        in_specs=[
            pl.BlockSpec((1, length, tile), lambda i: (i // per, 0, i % per)),
            pl.BlockSpec((1, runs, corrupted, tile), lambda i: (i // per, 0, 0, i % per)),
            whole(onehot.shape),
            pl.BlockSpec((1, taps_rows, tile), lambda i: (i // per, 0, i % per)),
            pl.BlockSpec((tile, width), lambda i: (i, 0)),
            *table_specs,
        ],
        out_specs=whole(((runs + 1) * length, width)),
        out_shape=jax.ShapeDtypeStruct(((runs + 1) * length, width), jnp.float32),
        compiler_params=pltpu.CompilerParams(vmem_limit_bytes=56 * 2**20),
    )(all_embed, all_noise, onehot, all_taps, out_weight, *tables)

    tile = min(256, width)
    return pl.pallas_call(
        second_kernel,
        grid=(width // tile,),
        in_specs=[
            pl.BlockSpec((length, tile), lambda i: (0, i)),
            pl.BlockSpec((runs, corrupted, tile), lambda i: (0, 0, i)),
            whole(onehot.shape),
            whole(flags.shape),
            pl.BlockSpec((taps_rows, tile), lambda i: (0, i)),
            pl.BlockSpec(((runs + 1) * length, tile), lambda i: (0, i)),
            *table_specs,
        ],
        out_specs=pl.BlockSpec((runs, length, tile), lambda i: (0, 0, i)),
        out_shape=jax.ShapeDtypeStruct((runs, length, width), jnp.bfloat16),
        compiler_params=pltpu.CompilerParams(vmem_limit_bytes=56 * 2**20),
    )(embed, noise, onehot, flags, taps_two, projected, *tables)


def solution(mesh):
    in_specs = (
        P("grp", "chan"),
        P(("grp", "run"), None, "chan"),
        P(("grp", "run"), None),
        P(("grp", "run"), None),
        P(None, "chan"),
        P(None, "chan"),
        P(None, "chan"),
        P(None, "chan"),
        P(None, "chan"),
    )
    out_specs = P(("grp", "run"), None, "chan")
    return jax.shard_map(
        per_device, mesh=mesh, in_specs=in_specs, out_specs=out_specs, check_vma=False
    )
```

```python
import functools

import jax
import jax.numpy as jnp
import numpy as np
from jax import lax
from jax.experimental import pallas as pl
from jax.experimental.pallas import tpu as pltpu
from jax.sharding import PartitionSpec as P


def transform_tables(length, taps_rows, size):
    half = size // 2
    angle = 2.0 * np.pi * (np.arange(half)[:, None] + 0.5) / size
    field = angle * np.arange(length)[None, :]
    taps = angle * np.arange(taps_rows)[None, :]
    forward = np.concatenate([np.cos(field), -np.sin(field)], axis=0)
    taps_forward = np.concatenate([np.cos(taps), -np.sin(taps)], axis=0)
    inverse = np.concatenate([np.cos(field), -np.sin(field)], axis=0).T * (2.0 / size)
    kinds = [jnp.asarray(table, dtype=jnp.bfloat16) for table in (forward, taps_forward, inverse)]
    return kinds


def dot(left, right):
    return jnp.dot(left, right, preferred_element_type=jnp.float32)


def gate(values):
    return 0.5 * values * (1.0 + jnp.tanh(0.5 * values))


def spectral_filter(field, spectrum_re, spectrum_im, forward, inverse):
    half = spectrum_re.shape[0]
    field_spectrum = dot(forward, field)
    re, im = field_spectrum[:half], field_spectrum[half:]
    out_re = (re * spectrum_re - im * spectrum_im).astype(jnp.bfloat16)
    out_im = (re * spectrum_im + im * spectrum_re).astype(jnp.bfloat16)
    return dot(inverse[:, :half], out_re) + dot(inverse[:, half:], out_im)


def exclusive_or(left, right, count):
    total, bit = 0, 1
    while bit < count:
        total = total + bit * ((left // bit + right // bit) % 2)
        bit *= 2
    return total


def project_kernel(
    chan_count, run_devices, per, length,
    own_ref, noise_ref, onehot, weight, forward, taps_forward, inverse, out,
    shared, noises, local_sem, z_send, z_recv, n_send, n_recv, x_send, x_recv, s_send, s_recv,
):
    step = pl.program_id(0)
    k = step // per
    j = step % per
    me = lax.axis_index("chan")
    run = lax.axis_index("run")
    row, core = run // 2, run % 2
    rows_x = run_devices // 2
    runs = onehot.shape[0]
    corrupted = onehot.shape[2]
    half = forward.shape[0] // 2
    rows_here = length // run_devices
    tile = weight.shape[0]
    mesh_ids = pl.DeviceIdType.MESH

    def remote(source, target, send, recv, device):
        return pltpu.make_async_remote_copy(
            src_ref=source, dst_ref=target, send_sem=send, recv_sem=recv,
            device_id=device, device_id_type=mesh_ids,
        )

    def to_chan(q):
        peer = {"chan": exclusive_or(me, q, chan_count)}
        slot = shared.at[me, run]
        return (
            remote(slot, slot, z_send.at[q], z_recv.at[q], peer),
            remote(noises.at[me], noises.at[me], n_send.at[q], n_recv.at[q], peer),
        )

    def from_chan(q):
        other = exclusive_or(me, q, chan_count)
        peer = {"chan": other}
        slot = shared.at[other, run]
        return (
            remote(slot, slot, z_send.at[q], z_recv.at[q], peer),
            remote(noises.at[other], noises.at[other], n_send.at[q], n_recv.at[q], peer),
        )

    def to_row(q, m):
        slot = shared.at[exclusive_or(me, q, chan_count), run]
        peer = {"run": ((row + m) % rows_x) * 2 + core}
        return remote(slot, slot, x_send.at[q, m], x_recv.at[q, m], peer)

    def from_row(q, m):
        source = ((row + rows_x - m) % rows_x) * 2 + core
        slot = shared.at[exclusive_or(me, q, chan_count), source]
        return remote(slot, slot, x_send.at[q, m], x_recv.at[q, m], {"run": source})

    def to_core(q, m):
        slot = shared.at[
            exclusive_or(me, q, chan_count), ((row + rows_x - m) % rows_x) * 2 + core
        ]
        return remote(slot, slot, s_send.at[q, m], s_recv.at[q, m], {"run": row * 2 + 1 - core})

    def from_core(q, m):
        slot = shared.at[
            exclusive_or(me, q, chan_count), ((row + rows_x - m) % rows_x) * 2 + 1 - core
        ]
        return remote(slot, slot, s_send.at[q, m], s_recv.at[q, m], {"run": row * 2 + 1 - core})

    @pl.when(step == 0)
    def _():
        first = pltpu.make_async_copy(own_ref, shared.at[me], local_sem.at[0])
        second = pltpu.make_async_copy(noise_ref, noises.at[me], local_sem.at[1])
        first.start()
        second.start()
        barrier = pltpu.get_barrier_semaphore()
        for q in range(1, chan_count):
            pl.semaphore_signal(
                barrier, inc=1, device_id={"chan": exclusive_or(me, q, chan_count)},
                device_id_type=mesh_ids,
            )
        for m in range(1, rows_x):
            pl.semaphore_signal(
                barrier, inc=1, device_id={"run": ((row + m) % rows_x) * 2 + core},
                device_id_type=mesh_ids,
            )
        pl.semaphore_signal(
            barrier, inc=1, device_id={"run": row * 2 + 1 - core}, device_id_type=mesh_ids
        )
        pl.semaphore_wait(barrier, chan_count - 1 + rows_x)
        first.wait()
        second.wait()
        out[...] = jnp.zeros_like(out)

    for q in range(1, chan_count):
        @pl.when(step == q - 1)
        def _():
            for copy in to_chan(q):
                copy.start()

    @pl.when((j == 0) & (k > 0))
    def _():
        for m in range(rows_x):
            from_core(k, m).wait_recv()
        from_chan(k)[1].wait_recv()

    @pl.when((j == per - 2) & (k < chan_count - 1))
    def _():
        from_chan(k + 1)[0].wait_recv()
        for m in range(1, rows_x):
            to_row(k + 1, m).start()
        to_core(k + 1, 0).start()

    @pl.when((j == per - 1) & (k < chan_count - 1))
    def _():
        for m in range(1, rows_x):
            from_row(k + 1, m).wait_recv()
            to_core(k + 1, m).start()

    source = exclusive_or(me, k, chan_count)
    columns = pl.ds(pl.multiple_of(j * tile, tile), tile)
    base = jnp.concatenate(
        [shared[source, r, :rows_here, columns] for r in range(run_devices)], axis=0
    )
    taps = jnp.concatenate(
        [shared[source, r, rows_here:, columns] for r in range(run_devices)], axis=0
    )
    spectrum = dot(taps_forward[...], taps)
    spectrum_re, spectrum_im = spectrum[:half], spectrum[half:]
    for r in range(runs + 1):
        if r < runs:
            added = dot(onehot[r], noises[source, r * corrupted:(r + 1) * corrupted, columns])
            field = (base.astype(jnp.float32) + added).astype(jnp.bfloat16)
        else:
            field = base
        filtered = spectral_filter(
            field, spectrum_re, spectrum_im, forward[...], inverse[...]
        )
        mixed = (filtered * gate(field.astype(jnp.float32))).astype(jnp.bfloat16)
        rows = pl.ds(r * length, length)
        out[rows] += dot(mixed, weight[...])

    @pl.when(step == chan_count * per - 1)
    def _():
        for q in range(1, chan_count):
            for copy in to_chan(q):
                copy.wait_send()
            for m in range(1, rows_x):
                to_row(q, m).wait_send()
            for m in range(rows_x):
                to_core(q, m).wait_send()


def second_kernel(
    embed, noise, onehot, restore, taps, projected, forward, taps_forward, inverse, out
):
    runs = noise.shape[0]
    length = embed.shape[0]
    half = forward.shape[0] // 2
    spectrum = dot(taps_forward[...], taps[...])
    spectrum_re, spectrum_im = spectrum[:half], spectrum[half:]
    base = embed[...].astype(jnp.float32)
    clean = (base + projected[pl.ds(runs * length, length)]).astype(jnp.bfloat16)
    for r in range(runs):
        added = dot(onehot[r], noise[r])
        field = (base + added).astype(jnp.bfloat16).astype(jnp.float32)
        hidden = (field + projected[pl.ds(r * length, length)]).astype(jnp.bfloat16)
        flags = restore[r]
        values = jnp.where(flags == 1, clean.astype(jnp.float32), hidden.astype(jnp.float32))
        second = spectral_filter(
            values.astype(jnp.bfloat16), spectrum_re, spectrum_im, forward[...], inverse[...]
        )
        out[r] = (values + second * gate(values)).astype(jnp.bfloat16)


def combined_taps(short_taps, long_taps, rows):
    total = jnp.zeros((rows, long_taps.shape[1]), jnp.float32)
    for k in range(short_taps.shape[0]):
        shifted = jnp.pad(long_taps, ((k, rows - k - long_taps.shape[0]), (0, 0)))
        total = total + short_taps[k][None, :] * shifted
    return total.astype(jnp.bfloat16)


def whole(shape):
    return pl.BlockSpec(shape, lambda *_: (0,) * len(shape))


def per_device(
    embed, noise, positions, restore, short_one, long_one, out_weight, short_two, long_two
):
    runs, corrupted, width = noise.shape
    length = embed.shape[0]
    chan_count = lax.axis_size("chan")
    run_devices = lax.axis_size("run")
    run_index = lax.axis_index("run")
    run_ids = run_index * runs + jnp.arange(runs, dtype=jnp.int32)
    span = short_one.shape[0] + long_one.shape[0] - 1
    unit = 16 * run_devices
    taps_rows = -(-span // unit) * unit
    size = 512
    assert length + span - 1 <= size
    forward, taps_forward, inverse = transform_tables(length, taps_rows, size)

    onehot = (
        (jnp.arange(length, dtype=jnp.int32)[None, :, None] == positions[:, None, :])
        & (run_ids != 0)[:, None, None]
    ).astype(jnp.bfloat16)
    block_size = length // restore.shape[1]
    flags = jnp.repeat(restore, block_size, axis=1)[:, :, None]

    taps_one = combined_taps(short_one, long_one, taps_rows)
    taps_two = combined_taps(short_two, long_two, taps_rows)

    rows_here = length // run_devices
    own = jnp.concatenate(
        [
            embed.reshape(run_devices, rows_here, width),
            taps_one.reshape(run_devices, taps_rows // run_devices, width),
        ],
        axis=1,
    )
    per = 4
    tile = width // per
    rows_x = run_devices // 2
    tables = [forward, taps_forward, inverse]
    table_specs = [whole(table.shape) for table in tables]
    anywhere = pl.BlockSpec(memory_space=pl.ANY)

    def weight_block(i):
        return exclusive_or(lax.axis_index("chan"), i // per, chan_count) * per + i % per, 0

    projected = pl.pallas_call(
        functools.partial(project_kernel, chan_count, run_devices, per, length),
        grid=(chan_count * per,),
        in_specs=[
            anywhere,
            anywhere,
            whole(onehot.shape),
            pl.BlockSpec((tile, width), weight_block),
            *table_specs,
        ],
        out_specs=whole(((runs + 1) * length, width)),
        out_shape=jax.ShapeDtypeStruct(((runs + 1) * length, width), jnp.float32),
        scratch_shapes=[
            pltpu.VMEM((chan_count, *own.shape), jnp.bfloat16),
            pltpu.VMEM((chan_count, runs * corrupted, width), jnp.bfloat16),
            pltpu.SemaphoreType.DMA((2,)),
            pltpu.SemaphoreType.DMA((chan_count,)),
            pltpu.SemaphoreType.DMA((chan_count,)),
            pltpu.SemaphoreType.DMA((chan_count,)),
            pltpu.SemaphoreType.DMA((chan_count,)),
            pltpu.SemaphoreType.DMA((chan_count, rows_x)),
            pltpu.SemaphoreType.DMA((chan_count, rows_x)),
            pltpu.SemaphoreType.DMA((chan_count, rows_x)),
            pltpu.SemaphoreType.DMA((chan_count, rows_x)),
        ],
        compiler_params=pltpu.CompilerParams(
            vmem_limit_bytes=56 * 2**20, collective_id=0, has_side_effects=True
        ),
    )(own, noise.reshape(runs * corrupted, width), onehot, out_weight, *tables)

    tile = min(256, width)
    return pl.pallas_call(
        second_kernel,
        grid=(width // tile,),
        in_specs=[
            pl.BlockSpec((length, tile), lambda i: (0, i)),
            pl.BlockSpec((runs, corrupted, tile), lambda i: (0, 0, i)),
            whole(onehot.shape),
            whole(flags.shape),
            pl.BlockSpec((taps_rows, tile), lambda i: (0, i)),
            pl.BlockSpec(((runs + 1) * length, tile), lambda i: (0, i)),
            *table_specs,
        ],
        out_specs=pl.BlockSpec((runs, length, tile), lambda i: (0, 0, i)),
        out_shape=jax.ShapeDtypeStruct((runs, length, width), jnp.bfloat16),
        compiler_params=pltpu.CompilerParams(vmem_limit_bytes=56 * 2**20),
    )(embed, noise, onehot, flags, taps_two, projected, *tables)


def solution(mesh):
    in_specs = (
        P("grp", "chan"),
        P(("grp", "run"), None, "chan"),
        P(("grp", "run"), None),
        P(("grp", "run"), None),
        P(None, "chan"),
        P(None, "chan"),
        P(None, "chan"),
        P(None, "chan"),
        P(None, "chan"),
    )
    out_specs = P(("grp", "run"), None, "chan")
    return jax.shard_map(
        per_device, mesh=mesh, in_specs=in_specs, out_specs=out_specs, check_vma=False
    )
```

```python
import functools

import jax
import jax.numpy as jnp
import numpy as np
from jax import lax
from jax.experimental import pallas as pl
from jax.experimental.pallas import tpu as pltpu
from jax.sharding import PartitionSpec as P


def transform_tables(length, taps_rows, size):
    half = size // 2
    angle = 2.0 * np.pi * (np.arange(half)[:, None] + 0.5) / size
    field = angle * np.arange(length)[None, :]
    taps = angle * np.arange(taps_rows)[None, :]
    forward = np.concatenate([np.cos(field), -np.sin(field)], axis=0)
    taps_forward = np.concatenate([np.cos(taps), -np.sin(taps)], axis=0)
    inverse = np.concatenate([np.cos(field), -np.sin(field)], axis=0).T * (2.0 / size)
    kinds = [jnp.asarray(table, dtype=jnp.bfloat16) for table in (forward, taps_forward, inverse)]
    return kinds


def dot(left, right):
    return jnp.dot(left, right, preferred_element_type=jnp.float32)


def gate(values):
    return 0.5 * values * (1.0 + jnp.tanh(0.5 * values))


def spectral_filter(field, spectrum_re, spectrum_im, forward, inverse):
    half = spectrum_re.shape[0]
    field_spectrum = dot(forward, field)
    re, im = field_spectrum[:half], field_spectrum[half:]
    out_re = (re * spectrum_re - im * spectrum_im).astype(jnp.bfloat16)
    out_im = (re * spectrum_im + im * spectrum_re).astype(jnp.bfloat16)
    return dot(inverse[:, :half], out_re) + dot(inverse[:, half:], out_im)


def exclusive_or(left, right, count):
    total, bit = 0, 1
    while bit < count:
        total = total + bit * ((left // bit + right // bit) % 2)
        bit *= 2
    return total


def project_kernel(
    chan_count, run_devices, per, length,
    own_ref, noise_ref, onehot, weight, forward, taps_forward, inverse, out,
    shared, noises, local_sem, z_send, z_recv, n_send, n_recv, x_send, x_recv, s_send, s_recv,
):
    step = pl.program_id(0)
    k = step // per
    j = step % per
    me = lax.axis_index("chan")
    run = lax.axis_index("run")
    row, core = run // 2, run % 2
    rows_x = run_devices // 2
    runs = onehot.shape[0]
    corrupted = onehot.shape[2]
    half = forward.shape[0] // 2
    rows_here = length // run_devices
    tile = weight.shape[0]
    mesh_ids = pl.DeviceIdType.MESH

    def remote(source, target, send, recv, device):
        return pltpu.make_async_remote_copy(
            src_ref=source, dst_ref=target, send_sem=send, recv_sem=recv,
            device_id=device, device_id_type=mesh_ids,
        )

    def to_chan(q):
        peer = {"chan": exclusive_or(me, q, chan_count)}
        slot = shared.at[me, run]
        return (
            remote(slot, slot, z_send.at[q], z_recv.at[q], peer),
            remote(noises.at[me], noises.at[me], n_send.at[q], n_recv.at[q], peer),
        )

    def pass_on(q):
        chunk = exclusive_or(me, q - 1, chan_count)
        peer = {"chan": exclusive_or(me, 1, chan_count)}
        slot = shared.at[chunk, run]
        return (
            remote(slot, slot, z_send.at[q], z_recv.at[q], peer),
            remote(noises.at[chunk], noises.at[chunk], n_send.at[q], n_recv.at[q], peer),
        )

    def from_chan(q):
        other = exclusive_or(me, q, chan_count)
        peer = {"chan": other}
        slot = shared.at[other, run]
        return (
            remote(slot, slot, z_send.at[q], z_recv.at[q], peer),
            remote(noises.at[other], noises.at[other], n_send.at[q], n_recv.at[q], peer),
        )

    def to_row(q, m):
        slot = shared.at[exclusive_or(me, q, chan_count), run]
        peer = {"run": ((row + m) % rows_x) * 2 + core}
        return remote(slot, slot, x_send.at[q, m], x_recv.at[q, m], peer)

    def from_row(q, m):
        source = ((row + rows_x - m) % rows_x) * 2 + core
        slot = shared.at[exclusive_or(me, q, chan_count), source]
        return remote(slot, slot, x_send.at[q, m], x_recv.at[q, m], {"run": source})

    def to_core(q, m):
        slot = shared.at[
            exclusive_or(me, q, chan_count), ((row + rows_x - m) % rows_x) * 2 + core
        ]
        return remote(slot, slot, s_send.at[q, m], s_recv.at[q, m], {"run": row * 2 + 1 - core})

    def from_core(q, m):
        slot = shared.at[
            exclusive_or(me, q, chan_count), ((row + rows_x - m) % rows_x) * 2 + 1 - core
        ]
        return remote(slot, slot, s_send.at[q, m], s_recv.at[q, m], {"run": row * 2 + 1 - core})

    @pl.when(step == 0)
    def _():
        first = pltpu.make_async_copy(own_ref, shared.at[me], local_sem.at[0])
        second = pltpu.make_async_copy(noise_ref, noises.at[me], local_sem.at[1])
        first.start()
        second.start()
        barrier = pltpu.get_barrier_semaphore()
        for q in range(1, chan_count):
            pl.semaphore_signal(
                barrier, inc=1, device_id={"chan": exclusive_or(me, q, chan_count)},
                device_id_type=mesh_ids,
            )
        for m in range(1, rows_x):
            pl.semaphore_signal(
                barrier, inc=1, device_id={"run": ((row + m) % rows_x) * 2 + core},
                device_id_type=mesh_ids,
            )
        pl.semaphore_signal(
            barrier, inc=1, device_id={"run": row * 2 + 1 - core}, device_id_type=mesh_ids
        )
        pl.semaphore_wait(barrier, chan_count - 1 + rows_x)
        first.wait()
        second.wait()
        out[...] = jnp.zeros_like(out)

    direct = [q for q in range(1, chan_count) if q == 1 or q % 2 == 0]
    for q in direct:
        @pl.when(step == q - 1)
        def _():
            for copy in to_chan(q):
                copy.start()

    @pl.when((j == 0) & (k > 0))
    def _():
        for m in range(rows_x):
            from_core(k, m).wait_recv()

    @pl.when((j == per - 2) & (k < chan_count - 1))
    def _():
        for copy in from_chan(k + 1):
            copy.wait_recv()
        for m in range(1, rows_x):
            to_row(k + 1, m).start()
        to_core(k + 1, 0).start()

    @pl.when((j == per - 2) & (k % 2 == 1) & (k < chan_count - 2))
    def _():
        for copy in pass_on(k + 2):
            copy.start()

    @pl.when((j == per - 1) & (k < chan_count - 1))
    def _():
        for m in range(1, rows_x):
            from_row(k + 1, m).wait_recv()
            to_core(k + 1, m).start()

    source = exclusive_or(me, k, chan_count)
    columns = pl.ds(pl.multiple_of(j * tile, tile), tile)
    base = jnp.concatenate(
        [shared[source, r, :rows_here, columns] for r in range(run_devices)], axis=0
    )
    taps = jnp.concatenate(
        [shared[source, r, rows_here:, columns] for r in range(run_devices)], axis=0
    )
    spectrum = dot(taps_forward[...], taps)
    spectrum_re, spectrum_im = spectrum[:half], spectrum[half:]
    for r in range(runs + 1):
        if r < runs:
            added = dot(onehot[r], noises[source, r * corrupted:(r + 1) * corrupted, columns])
            field = (base.astype(jnp.float32) + added).astype(jnp.bfloat16)
        else:
            field = base
        filtered = spectral_filter(
            field, spectrum_re, spectrum_im, forward[...], inverse[...]
        )
        mixed = (filtered * gate(field.astype(jnp.float32))).astype(jnp.bfloat16)
        rows = pl.ds(r * length, length)
        out[rows] += dot(mixed, weight[...])

    @pl.when(step == chan_count * per - 1)
    def _():
        for q in range(1, chan_count):
            for copy in to_chan(q) if q in direct else pass_on(q):
                copy.wait_send()
            for m in range(1, rows_x):
                to_row(q, m).wait_send()
            for m in range(rows_x):
                to_core(q, m).wait_send()


def second_kernel(
    embed, noise, onehot, restore, taps, projected, forward, taps_forward, inverse, out
):
    runs = noise.shape[0]
    length = embed.shape[0]
    half = forward.shape[0] // 2
    spectrum = dot(taps_forward[...], taps[...])
    spectrum_re, spectrum_im = spectrum[:half], spectrum[half:]
    base = embed[...].astype(jnp.float32)
    clean = (base + projected[pl.ds(runs * length, length)]).astype(jnp.bfloat16)
    for r in range(runs):
        added = dot(onehot[r], noise[r])
        field = (base + added).astype(jnp.bfloat16).astype(jnp.float32)
        hidden = (field + projected[pl.ds(r * length, length)]).astype(jnp.bfloat16)
        flags = restore[r]
        values = jnp.where(flags == 1, clean.astype(jnp.float32), hidden.astype(jnp.float32))
        second = spectral_filter(
            values.astype(jnp.bfloat16), spectrum_re, spectrum_im, forward[...], inverse[...]
        )
        out[r] = (values + second * gate(values)).astype(jnp.bfloat16)


def combined_taps(short_taps, long_taps, rows):
    total = jnp.zeros((rows, long_taps.shape[1]), jnp.float32)
    for k in range(short_taps.shape[0]):
        shifted = jnp.pad(long_taps, ((k, rows - k - long_taps.shape[0]), (0, 0)))
        total = total + short_taps[k][None, :] * shifted
    return total.astype(jnp.bfloat16)


def whole(shape):
    return pl.BlockSpec(shape, lambda *_: (0,) * len(shape))


def per_device(
    embed, noise, positions, restore, short_one, long_one, out_weight, short_two, long_two
):
    runs, corrupted, width = noise.shape
    length = embed.shape[0]
    chan_count = lax.axis_size("chan")
    run_devices = lax.axis_size("run")
    run_index = lax.axis_index("run")
    run_ids = run_index * runs + jnp.arange(runs, dtype=jnp.int32)
    span = short_one.shape[0] + long_one.shape[0] - 1
    unit = 16 * run_devices
    taps_rows = -(-span // unit) * unit
    size = 512
    assert length + span - 1 <= size
    forward, taps_forward, inverse = transform_tables(length, taps_rows, size)

    onehot = (
        (jnp.arange(length, dtype=jnp.int32)[None, :, None] == positions[:, None, :])
        & (run_ids != 0)[:, None, None]
    ).astype(jnp.bfloat16)
    block_size = length // restore.shape[1]
    flags = jnp.repeat(restore, block_size, axis=1)[:, :, None]

    taps_one = combined_taps(short_one, long_one, taps_rows)
    taps_two = combined_taps(short_two, long_two, taps_rows)

    rows_here = length // run_devices
    own = jnp.concatenate(
        [
            embed.reshape(run_devices, rows_here, width),
            taps_one.reshape(run_devices, taps_rows // run_devices, width),
        ],
        axis=1,
    )
    per = 4
    tile = width // per
    rows_x = run_devices // 2
    tables = [forward, taps_forward, inverse]
    table_specs = [whole(table.shape) for table in tables]
    anywhere = pl.BlockSpec(memory_space=pl.ANY)

    def weight_block(i):
        return exclusive_or(lax.axis_index("chan"), i // per, chan_count) * per + i % per, 0

    projected = pl.pallas_call(
        functools.partial(project_kernel, chan_count, run_devices, per, length),
        grid=(chan_count * per,),
        in_specs=[
            anywhere,
            anywhere,
            whole(onehot.shape),
            pl.BlockSpec((tile, width), weight_block),
            *table_specs,
        ],
        out_specs=whole(((runs + 1) * length, width)),
        out_shape=jax.ShapeDtypeStruct(((runs + 1) * length, width), jnp.float32),
        scratch_shapes=[
            pltpu.VMEM((chan_count, *own.shape), jnp.bfloat16),
            pltpu.VMEM((chan_count, runs * corrupted, width), jnp.bfloat16),
            pltpu.SemaphoreType.DMA((2,)),
            pltpu.SemaphoreType.DMA((chan_count,)),
            pltpu.SemaphoreType.DMA((chan_count,)),
            pltpu.SemaphoreType.DMA((chan_count,)),
            pltpu.SemaphoreType.DMA((chan_count,)),
            pltpu.SemaphoreType.DMA((chan_count, rows_x)),
            pltpu.SemaphoreType.DMA((chan_count, rows_x)),
            pltpu.SemaphoreType.DMA((chan_count, rows_x)),
            pltpu.SemaphoreType.DMA((chan_count, rows_x)),
        ],
        compiler_params=pltpu.CompilerParams(
            vmem_limit_bytes=56 * 2**20, collective_id=0, has_side_effects=True
        ),
    )(own, noise.reshape(runs * corrupted, width), onehot, out_weight, *tables)

    tile = min(256, width)
    return pl.pallas_call(
        second_kernel,
        grid=(width // tile,),
        in_specs=[
            pl.BlockSpec((length, tile), lambda i: (0, i)),
            pl.BlockSpec((runs, corrupted, tile), lambda i: (0, 0, i)),
            whole(onehot.shape),
            whole(flags.shape),
            pl.BlockSpec((taps_rows, tile), lambda i: (0, i)),
            pl.BlockSpec(((runs + 1) * length, tile), lambda i: (0, i)),
            *table_specs,
        ],
        out_specs=pl.BlockSpec((runs, length, tile), lambda i: (0, 0, i)),
        out_shape=jax.ShapeDtypeStruct((runs, length, width), jnp.bfloat16),
        compiler_params=pltpu.CompilerParams(vmem_limit_bytes=56 * 2**20),
    )(embed, noise, onehot, flags, taps_two, projected, *tables)


def solution(mesh):
    in_specs = (
        P("grp", "chan"),
        P(("grp", "run"), None, "chan"),
        P(("grp", "run"), None),
        P(("grp", "run"), None),
        P(None, "chan"),
        P(None, "chan"),
        P(None, "chan"),
        P(None, "chan"),
        P(None, "chan"),
    )
    out_specs = P(("grp", "run"), None, "chan")
    return jax.shard_map(
        per_device, mesh=mesh, in_specs=in_specs, out_specs=out_specs, check_vma=False
    )
```

```python
import functools

import jax
import jax.numpy as jnp
import numpy as np
from jax import lax
from jax.experimental import pallas as pl
from jax.experimental.pallas import tpu as pltpu
from jax.sharding import PartitionSpec as P


def transform_tables(length, taps_rows, size):
    half = size // 2
    angle = 2.0 * np.pi * (np.arange(half)[:, None] + 0.5) / size
    field = angle * np.arange(length)[None, :]
    taps = angle * np.arange(taps_rows)[None, :]
    forward = np.concatenate([np.cos(field), -np.sin(field)], axis=0)
    taps_forward = np.concatenate([np.cos(taps), -np.sin(taps)], axis=0)
    inverse = np.concatenate([np.cos(field), -np.sin(field)], axis=0).T * (2.0 / size)
    kinds = [jnp.asarray(table, dtype=jnp.bfloat16) for table in (forward, taps_forward, inverse)]
    return kinds


def dot(left, right):
    return jnp.dot(left, right, preferred_element_type=jnp.float32)


def gate(values):
    return 0.5 * values * (1.0 + jnp.tanh(0.5 * values))


def spectral_filter(field, spectrum_re, spectrum_im, forward, inverse):
    half = spectrum_re.shape[0]
    field_spectrum = dot(forward, field)
    re, im = field_spectrum[:half], field_spectrum[half:]
    out_re = (re * spectrum_re - im * spectrum_im).astype(jnp.bfloat16)
    out_im = (re * spectrum_im + im * spectrum_re).astype(jnp.bfloat16)
    return dot(inverse[:, :half], out_re) + dot(inverse[:, half:], out_im)


def exclusive_or(left, right, count):
    total, bit = 0, 1
    while bit < count:
        total = total + bit * ((left // bit + right // bit) % 2)
        bit *= 2
    return total


def project_kernel(
    chan_count, run_devices, per, length,
    own_ref, noise_ref, onehot, weight, forward, taps_forward, inverse, out,
    shared, noises, local_sem, z_send, z_recv, n_send, n_recv, x_send, x_recv, s_send, s_recv,
):
    step = pl.program_id(0)
    k = step // per
    j = step % per
    me = lax.axis_index("chan")
    run = lax.axis_index("run")
    row, core = run // 2, run % 2
    rows_x = run_devices // 2
    runs = onehot.shape[0]
    corrupted = onehot.shape[2]
    half = forward.shape[0] // 2
    rows_here = length // run_devices
    tile = weight.shape[0]
    mesh_ids = pl.DeviceIdType.MESH

    def remote(source, target, send, recv, device):
        return pltpu.make_async_remote_copy(
            src_ref=source, dst_ref=target, send_sem=send, recv_sem=recv,
            device_id=device, device_id_type=mesh_ids,
        )

    def to_chan(q):
        peer = {"chan": exclusive_or(me, q, chan_count)}
        slot = shared.at[me, run]
        return (
            remote(slot, slot, z_send.at[q], z_recv.at[q], peer),
            remote(noises.at[me], noises.at[me], n_send.at[q], n_recv.at[q], peer),
        )

    def from_chan(q):
        other = exclusive_or(me, q, chan_count)
        peer = {"chan": other}
        slot = shared.at[other, run]
        return (
            remote(slot, slot, z_send.at[q], z_recv.at[q], peer),
            remote(noises.at[other], noises.at[other], n_send.at[q], n_recv.at[q], peer),
        )

    def to_row(q, m):
        slot = shared.at[exclusive_or(me, q, chan_count), run]
        peer = {"run": ((row + m) % rows_x) * 2 + core}
        return remote(slot, slot, x_send.at[q, m], x_recv.at[q, m], peer)

    def from_row(q, m):
        source = ((row + rows_x - m) % rows_x) * 2 + core
        slot = shared.at[exclusive_or(me, q, chan_count), source]
        return remote(slot, slot, x_send.at[q, m], x_recv.at[q, m], {"run": source})

    def to_core(q, m):
        slot = shared.at[
            exclusive_or(me, q, chan_count), ((row + rows_x - m) % rows_x) * 2 + core
        ]
        return remote(slot, slot, s_send.at[q, m], s_recv.at[q, m], {"run": row * 2 + 1 - core})

    def from_core(q, m):
        slot = shared.at[
            exclusive_or(me, q, chan_count), ((row + rows_x - m) % rows_x) * 2 + 1 - core
        ]
        return remote(slot, slot, s_send.at[q, m], s_recv.at[q, m], {"run": row * 2 + 1 - core})

    @pl.when(step == 0)
    def _():
        first = pltpu.make_async_copy(own_ref, shared.at[me], local_sem.at[0])
        second = pltpu.make_async_copy(noise_ref, noises.at[me], local_sem.at[1])
        first.start()
        second.start()
        barrier = pltpu.get_barrier_semaphore()
        for q in range(1, chan_count):
            pl.semaphore_signal(
                barrier, inc=1, device_id={"chan": exclusive_or(me, q, chan_count)},
                device_id_type=mesh_ids,
            )
        for m in range(1, rows_x):
            pl.semaphore_signal(
                barrier, inc=1, device_id={"run": ((row + m) % rows_x) * 2 + core},
                device_id_type=mesh_ids,
            )
        pl.semaphore_signal(
            barrier, inc=1, device_id={"run": row * 2 + 1 - core}, device_id_type=mesh_ids
        )
        pl.semaphore_wait(barrier, chan_count - 1 + rows_x)
        first.wait()
        second.wait()
        out[...] = jnp.zeros_like(out)

    for q in range(1, chan_count):
        @pl.when(step == q - 1)
        def _():
            for copy in to_chan(q):
                copy.start()

    @pl.when((j == 0) & (k > 0))
    def _():
        for m in range(rows_x):
            from_core(k, m).wait_recv()
        from_chan(k)[1].wait_recv()

    @pl.when((j == per - 3) & (k < chan_count - 1))
    def _():
        from_chan(k + 1)[0].wait_recv()
        for m in range(1, rows_x):
            to_row(k + 1, m).start()
        to_core(k + 1, 0).start()

    @pl.when((j == per - 2) & (k < chan_count - 1))
    def _():
        for m in range(1, rows_x):
            from_row(k + 1, m).wait_recv()
            to_core(k + 1, m).start()

    source = exclusive_or(me, k, chan_count)
    columns = pl.ds(pl.multiple_of(j * tile, tile), tile)
    base = jnp.concatenate(
        [shared[source, r, :rows_here, columns] for r in range(run_devices)], axis=0
    )
    taps = jnp.concatenate(
        [shared[source, r, rows_here:, columns] for r in range(run_devices)], axis=0
    )
    spectrum = dot(taps_forward[...], taps)
    spectrum_re, spectrum_im = spectrum[:half], spectrum[half:]
    for r in range(runs + 1):
        if r < runs:
            added = dot(onehot[r], noises[source, r * corrupted:(r + 1) * corrupted, columns])
            field = (base.astype(jnp.float32) + added).astype(jnp.bfloat16)
        else:
            field = base
        filtered = spectral_filter(
            field, spectrum_re, spectrum_im, forward[...], inverse[...]
        )
        mixed = (filtered * gate(field.astype(jnp.float32))).astype(jnp.bfloat16)
        rows = pl.ds(r * length, length)
        out[rows] += dot(mixed, weight[...])

    @pl.when(step == chan_count * per - 1)
    def _():
        for q in range(1, chan_count):
            for copy in to_chan(q):
                copy.wait_send()
            for m in range(1, rows_x):
                to_row(q, m).wait_send()
            for m in range(rows_x):
                to_core(q, m).wait_send()


def second_kernel(
    embed, noise, onehot, restore, taps, projected, forward, taps_forward, inverse, out
):
    runs = noise.shape[0]
    length = embed.shape[0]
    half = forward.shape[0] // 2
    spectrum = dot(taps_forward[...], taps[...])
    spectrum_re, spectrum_im = spectrum[:half], spectrum[half:]
    base = embed[...].astype(jnp.float32)
    clean = (base + projected[pl.ds(runs * length, length)]).astype(jnp.bfloat16)
    for r in range(runs):
        added = dot(onehot[r], noise[r])
        field = (base + added).astype(jnp.bfloat16).astype(jnp.float32)
        hidden = (field + projected[pl.ds(r * length, length)]).astype(jnp.bfloat16)
        flags = restore[r]
        values = jnp.where(flags == 1, clean.astype(jnp.float32), hidden.astype(jnp.float32))
        second = spectral_filter(
            values.astype(jnp.bfloat16), spectrum_re, spectrum_im, forward[...], inverse[...]
        )
        out[r] = (values + second * gate(values)).astype(jnp.bfloat16)


def combined_taps(short_taps, long_taps, rows):
    total = jnp.zeros((rows, long_taps.shape[1]), jnp.float32)
    for k in range(short_taps.shape[0]):
        shifted = jnp.pad(long_taps, ((k, rows - k - long_taps.shape[0]), (0, 0)))
        total = total + short_taps[k][None, :] * shifted
    return total.astype(jnp.bfloat16)


def whole(shape):
    return pl.BlockSpec(shape, lambda *_: (0,) * len(shape))


def per_device(
    embed, noise, positions, restore, short_one, long_one, out_weight, short_two, long_two
):
    runs, corrupted, width = noise.shape
    length = embed.shape[0]
    chan_count = lax.axis_size("chan")
    run_devices = lax.axis_size("run")
    run_index = lax.axis_index("run")
    run_ids = run_index * runs + jnp.arange(runs, dtype=jnp.int32)
    span = short_one.shape[0] + long_one.shape[0] - 1
    unit = 16 * run_devices
    taps_rows = -(-span // unit) * unit
    size = 512
    assert length + span - 1 <= size
    forward, taps_forward, inverse = transform_tables(length, taps_rows, size)

    onehot = (
        (jnp.arange(length, dtype=jnp.int32)[None, :, None] == positions[:, None, :])
        & (run_ids != 0)[:, None, None]
    ).astype(jnp.bfloat16)
    block_size = length // restore.shape[1]
    flags = jnp.repeat(restore, block_size, axis=1)[:, :, None]

    taps_one = combined_taps(short_one, long_one, taps_rows)
    taps_two = combined_taps(short_two, long_two, taps_rows)

    rows_here = length // run_devices
    own = jnp.concatenate(
        [
            embed.reshape(run_devices, rows_here, width),
            taps_one.reshape(run_devices, taps_rows // run_devices, width),
        ],
        axis=1,
    )
    per = 4
    tile = width // per
    rows_x = run_devices // 2
    tables = [forward, taps_forward, inverse]
    table_specs = [whole(table.shape) for table in tables]
    anywhere = pl.BlockSpec(memory_space=pl.ANY)

    def weight_block(i):
        return exclusive_or(lax.axis_index("chan"), i // per, chan_count) * per + i % per, 0

    projected = pl.pallas_call(
        functools.partial(project_kernel, chan_count, run_devices, per, length),
        grid=(chan_count * per,),
        in_specs=[
            anywhere,
            anywhere,
            whole(onehot.shape),
            pl.BlockSpec((tile, width), weight_block),
            *table_specs,
        ],
        out_specs=whole(((runs + 1) * length, width)),
        out_shape=jax.ShapeDtypeStruct(((runs + 1) * length, width), jnp.float32),
        scratch_shapes=[
            pltpu.VMEM((chan_count, *own.shape), jnp.bfloat16),
            pltpu.VMEM((chan_count, runs * corrupted, width), jnp.bfloat16),
            pltpu.SemaphoreType.DMA((2,)),
            pltpu.SemaphoreType.DMA((chan_count,)),
            pltpu.SemaphoreType.DMA((chan_count,)),
            pltpu.SemaphoreType.DMA((chan_count,)),
            pltpu.SemaphoreType.DMA((chan_count,)),
            pltpu.SemaphoreType.DMA((chan_count, rows_x)),
            pltpu.SemaphoreType.DMA((chan_count, rows_x)),
            pltpu.SemaphoreType.DMA((chan_count, rows_x)),
            pltpu.SemaphoreType.DMA((chan_count, rows_x)),
        ],
        compiler_params=pltpu.CompilerParams(
            vmem_limit_bytes=56 * 2**20, collective_id=0, has_side_effects=True
        ),
    )(own, noise.reshape(runs * corrupted, width), onehot, out_weight, *tables)

    tile = min(256, width)
    return pl.pallas_call(
        second_kernel,
        grid=(width // tile,),
        in_specs=[
            pl.BlockSpec((length, tile), lambda i: (0, i)),
            pl.BlockSpec((runs, corrupted, tile), lambda i: (0, 0, i)),
            whole(onehot.shape),
            whole(flags.shape),
            pl.BlockSpec((taps_rows, tile), lambda i: (0, i)),
            pl.BlockSpec(((runs + 1) * length, tile), lambda i: (0, i)),
            *table_specs,
        ],
        out_specs=pl.BlockSpec((runs, length, tile), lambda i: (0, 0, i)),
        out_shape=jax.ShapeDtypeStruct((runs, length, width), jnp.bfloat16),
        compiler_params=pltpu.CompilerParams(vmem_limit_bytes=56 * 2**20),
    )(embed, noise, onehot, flags, taps_two, projected, *tables)


def solution(mesh):
    in_specs = (
        P("grp", "chan"),
        P(("grp", "run"), None, "chan"),
        P(("grp", "run"), None),
        P(("grp", "run"), None),
        P(None, "chan"),
        P(None, "chan"),
        P(None, "chan"),
        P(None, "chan"),
        P(None, "chan"),
    )
    out_specs = P(("grp", "run"), None, "chan")
    return jax.shard_map(
        per_device, mesh=mesh, in_specs=in_specs, out_specs=out_specs, check_vma=False
    )
```
